32 devices in a mesh: dp: 4 (over y, x), seq: 8 (over z, core).
Axes of the slice: x: 2, y: 2, z: 4, core: 2. Of those that a mesh axis runs over, the one named last changes fastest.
Arguments:
- queries: bfloat16 [4096, 4096], P(('dp', 'seq')), may hold values from -30 to 30
- keys: bfloat16 [4096, 512], P(('dp', 'seq')), may hold values from -7.5 to 7.5
- values: bfloat16 [4096, 512], P(('dp', 'seq')), may hold values from -4 to 4
- doc_lengths: int32 [4, 32], replicated, may hold values from 0 to 128, as said below
- loader_order: int32 [4, 4], replicated, may hold values from 0 to 3, each once within a row
- grad_out: bfloat16 [4096, 4096], P(('dp', 'seq')), may hold values from -4 to 4
Outputs:
- attended: bfloat16 [4096, 4096], P(('dp', 'seq'))
- grad_queries: bfloat16 [4096, 4096], P(('dp', 'seq'))
- grad_keys: bfloat16 [4096, 512], P(('dp', 'seq'))
- grad_values: bfloat16 [4096, 512], P(('dp', 'seq'))
The draws below stay inside these ranges and needn't reach their ends.
Inputs may be any that keep to these rules, and one draw needn't show every extreme that they name: `doc_lengths`: the documents of a bin fill its first positions in order; each is 32 to 128 long except that a bin's last may be shorter, and the entries after it are 0. The first document of every bin is 128 long; every bin holds 512 tokens or more, and some bin exactly 1024.
All inputs are finite; a program needn't handle non-finite values.
Results may differ from the reference program's by a relative error of at most 0.0067.
Values may be sent and summed in bfloat16 or wider, within the bound.
A program may use at most 64 MiB of HBM per device.

```python
import jax
import jax.numpy as jnp
from jax import lax

QH = 32
KVH = 4
HD = 128
GROUP = 8
LOAD = 1024
CAP = 256
BLOCK = 128
DOC_MOST = 128
DOC_LEAST = 32
DOCS = 32
TOKENS = 4096
N_DP = 4


def shared_keys(key):
    key_base = jnp.clip(jax.random.normal(key, (TOKENS, KVH * HD), jnp.float32), -4.0, 4.0)
    return key_base


def draw_doc_lengths(key, part):
    key = jax.random.fold_in(key, 11)
    first_key, second_key, third_key = jax.random.split(key, 3)
    drawn_lengths = jax.random.randint(first_key, (N_DP, DOCS), DOC_LEAST, DOC_MOST + 1)
    drawn_lengths = drawn_lengths.at[:, 0].set(DOC_MOST)
    bin_limit = jax.random.randint(second_key, (N_DP,), LOAD // 2, LOAD + 1)
    full_bin = jax.random.randint(third_key, (), 0, N_DP)
    bin_limit = jnp.where(jnp.arange(N_DP) == full_bin, LOAD, bin_limit)
    doc_starts = jnp.cumsum(drawn_lengths, axis=1) - drawn_lengths
    lengths = jnp.clip(bin_limit[:, None] - doc_starts, 0, drawn_lengths)
    return lengths.astype(jnp.int32)


def draw_keys(key, part):
    key_base = shared_keys(key)
    result = key_base
    return result.astype(jnp.bfloat16)


def draw_queries(key, part):
    key = jax.random.fold_in(key, 5)
    result = jnp.clip(jax.random.normal(key, (TOKENS, QH * HD), jnp.float32), -4.0, 4.0)
    return result.astype(jnp.bfloat16)


def levels(stream_key, shape, cuts, low, high):
    def one(axis_at, blocks):
        draws = jax.random.uniform(jax.random.fold_in(jax.random.fold_in(stream_key, 6), axis_at), (blocks,), jnp.float32, low / len(cuts), high / len(cuts))
        return jnp.repeat(jnp.exp(draws), shape[axis_at] // blocks).reshape((-1,) + (1,) * (len(shape) - axis_at - 1))

    level = one(*cuts[0])
    for cut in cuts[1:]:
        level = level * one(*cut)
    return level


def noise(key, dims, deviation, limit, pieces=(), held_as=jnp.bfloat16):
    factor_of = levels(key, dims, pieces, -0.22, 0.18) if pieces else 1.0
    values = jax.random.normal(key, dims, jnp.float32) * deviation * factor_of
    return jnp.minimum(jnp.maximum(values, -limit), limit).astype(held_as)


def setup_inputs(seed: int = 0) -> dict:
    key_of = jax.random.split(jax.random.key(seed), 7)
    queries = draw_queries(jax.random.fold_in(key_of[6], 71), 0)
    keys = draw_keys(jax.random.fold_in(key_of[6], 71), 0)
    values = noise(key_of[2], (TOKENS, KVH * HD), 1.0, 4.0, ((0, 32),))
    doc_lengths = draw_doc_lengths(jax.random.fold_in(key_of[6], 71), 0)
    loader_order = jax.vmap(lambda own: jax.random.permutation(own, N_DP))(jax.random.split(key_of[4], N_DP)).reshape((N_DP, N_DP)).astype(jnp.int32)
    grad_out = noise(key_of[5], (TOKENS, QH * HD), 1.0, 4.0, ((0, 32),))
    return {"queries": queries, "keys": keys, "values": values, "doc_lengths": doc_lengths, "loader_order": loader_order, "grad_out": grad_out}


def bin_layout(lengths, row_count):
    doc_ends = jnp.cumsum(lengths, axis=-1).astype(jnp.int32)
    filled_to = doc_ends[..., -1]
    positions = jnp.arange(row_count, dtype=jnp.int32)
    doc_of = jnp.sum((doc_ends[..., None, :] <= positions[:, None]).astype(jnp.int32), axis=-1).astype(jnp.int32)
    marked = jnp.where(positions < filled_to[..., None], doc_of, -1 - positions)
    return filled_to, marked


def loader_runs(filled_to, order_row, source, capacity):
    bin_index = jnp.arange(filled_to.shape[0], dtype=jnp.int32)
    counts = jnp.clip(filled_to - source * capacity, 0, capacity).astype(jnp.int32)
    choose_run = (order_row[:, None] == bin_index[None, :]).astype(jnp.int32)
    ordered = jnp.sum(choose_run * counts[None, :], axis=1).astype(jnp.int32)
    run_start = (jnp.cumsum(ordered) - ordered).astype(jnp.int32)
    return ordered, run_start


def loader_targets(ordered, run_start, order_row, capacity, row_count):
    positions = jnp.arange(row_count, dtype=jnp.int32)
    inside = (positions[:, None] >= run_start[None, :]) & (positions[:, None] < (run_start + ordered)[None, :])
    target = order_row * capacity - run_start
    slot_index = jnp.sum(jnp.where(inside, target[None, :], 0), axis=1).astype(jnp.int32) + positions
    return slot_index, jnp.any(inside, axis=1)


def rounded(array):
    return lax.optimization_barrier(array.astype(jnp.bfloat16)).astype(jnp.float32)


def one_bin(bin_items):
    bin_query, bin_keys, bin_values, marked, grad_bin = bin_items
    score_scale = HD ** -0.5
    keys_pad = jnp.concatenate([jnp.zeros((BLOCK, KVH, HD), jnp.float32), bin_keys.astype(jnp.float32)], axis=0)
    values_pad = jnp.concatenate([jnp.zeros((BLOCK, KVH, HD), jnp.float32), bin_values.astype(jnp.float32)], axis=0)
    marked_pad = jnp.concatenate([-2 * LOAD - jnp.arange(BLOCK, dtype=jnp.int32), marked]).astype(jnp.int32)
    query_rows = jnp.arange(BLOCK, dtype=jnp.int32)[:, None] + BLOCK
    window_cols = jnp.arange(2 * BLOCK, dtype=jnp.int32)[None, :]

    def tile(running, tile_number):
        key_total, value_total = running
        tile_start = tile_number * BLOCK
        query_tile = lax.dynamic_slice_in_dim(bin_query, tile_start, BLOCK, 0).astype(jnp.float32)
        grad_rows = lax.dynamic_slice_in_dim(grad_bin, tile_start, BLOCK, 0)
        marked_query = lax.dynamic_slice_in_dim(marked, tile_start, BLOCK, 0)
        keys_wide = jnp.repeat(lax.dynamic_slice_in_dim(keys_pad, tile_start, 2 * BLOCK, 0), GROUP, axis=1)
        values_wide = jnp.repeat(lax.dynamic_slice_in_dim(values_pad, tile_start, 2 * BLOCK, 0), GROUP, axis=1)
        marked_window = lax.dynamic_slice_in_dim(marked_pad, tile_start, 2 * BLOCK, 0)
        allowed = (marked_query[:, None] == marked_window[None, :]) & (window_cols <= query_rows)
        scores = jnp.einsum("qhd,khd->hqk", query_tile, keys_wide) * score_scale
        scores = jnp.where(allowed[None], scores, -jnp.inf)
        row_peak = jnp.max(scores, axis=-1, keepdims=True)
        row_total = jnp.sum(jnp.exp(scores - row_peak), axis=-1, keepdims=True)
        probs_full = jnp.exp(scores - (row_peak + jnp.log(row_total)))
        probs_half = rounded(probs_full)
        filled_slot = marked_query >= 0
        attended32 = jnp.einsum("hqk,khd->qhd", probs_half, values_wide)
        attended32 = jnp.where(filled_slot[:, None, None], attended32, jnp.float32(0.0))
        grad_here = jnp.where(filled_slot[:, None, None], grad_rows, jnp.zeros((), jnp.bfloat16)).astype(jnp.float32)
        grad_probs = jnp.einsum("qhd,khd->hqk", grad_here, values_wide)
        row_dot = jnp.transpose(jnp.sum(grad_here * attended32, axis=-1), (1, 0))[..., None]
        grad_half = rounded(probs_full * (grad_probs - row_dot))
        grad_query = jnp.einsum("hqk,khd->qhd", grad_half, keys_wide) * score_scale
        key_terms = jnp.einsum("hqk,qhd->khd", grad_half, query_tile) * score_scale
        value_terms = jnp.einsum("hqk,qhd->khd", probs_half, grad_here)
        key_terms = jnp.sum(key_terms.reshape(2 * BLOCK, KVH, GROUP, HD), axis=2)
        value_terms = jnp.sum(value_terms.reshape(2 * BLOCK, KVH, GROUP, HD), axis=2)
        key_total = lax.dynamic_update_slice_in_dim(key_total, lax.dynamic_slice_in_dim(key_total, tile_start, 2 * BLOCK, 0) + key_terms, tile_start, 0)
        value_total = lax.dynamic_update_slice_in_dim(value_total, lax.dynamic_slice_in_dim(value_total, tile_start, 2 * BLOCK, 0) + value_terms, tile_start, 0)
        return (key_total, value_total), (attended32.astype(jnp.bfloat16).reshape(BLOCK, QH * HD), grad_query.astype(jnp.bfloat16).reshape(BLOCK, QH * HD))

    empty_total = jnp.zeros((BLOCK + LOAD, KVH, HD), jnp.float32)
    totals, tiles_out = lax.scan(tile, (empty_total, empty_total), jnp.arange(8, dtype=jnp.int32))
    return (tiles_out[0].reshape(LOAD, QH * HD),
            tiles_out[1].reshape(LOAD, QH * HD),
            totals[0][BLOCK:].astype(jnp.bfloat16).reshape(LOAD, KVH * HD),
            totals[1][BLOCK:].astype(jnp.bfloat16).reshape(LOAD, KVH * HD))


def reference(queries, keys, values, doc_lengths, loader_order, grad_out):
    filled_to, marked = bin_layout(doc_lengths, LOAD)
    sources = jnp.arange(N_DP, dtype=jnp.int32)
    ordered, run_start = jax.vmap(loader_runs, in_axes=(None, 0, 0, None))(filled_to, loader_order, sources, CAP)
    slot_index, placed = jax.vmap(loader_targets, in_axes=(0, 0, 0, None, None))(ordered, run_start, loader_order, CAP, LOAD)
    target_row = (slot_index // CAP) * LOAD + sources[:, None] * CAP + slot_index % CAP
    target_row = jnp.where(placed, target_row, N_DP * LOAD).reshape(-1).astype(jnp.int32)
    bin_query = jnp.zeros((N_DP * LOAD, QH * HD), jnp.bfloat16).at[target_row].set(queries, mode="drop")
    bin_keys = jnp.zeros((N_DP * LOAD, KVH * HD), jnp.bfloat16).at[target_row].set(keys, mode="drop")
    bin_values = jnp.zeros((N_DP * LOAD, KVH * HD), jnp.bfloat16).at[target_row].set(values, mode="drop")
    bin_items = (bin_query.reshape(N_DP, LOAD, QH, HD),
                 bin_keys.reshape(N_DP, LOAD, KVH, HD),
                 bin_values.reshape(N_DP, LOAD, KVH, HD),
                 marked,
                 grad_out.reshape(N_DP, LOAD, QH, HD))
    attended, grad_queries, grad_keys, grad_values = lax.map(one_bin, bin_items)
    return (attended.reshape(N_DP * LOAD, QH * HD),
            grad_queries.reshape(N_DP * LOAD, QH * HD),
            grad_keys.reshape(N_DP * LOAD, KVH * HD),
            grad_values.reshape(N_DP * LOAD, KVH * HD))
```

```python
import functools

import jax
import jax.numpy as jnp
from jax import lax
from jax.experimental import pallas as pl
from jax.experimental.pallas import tpu as pltpu
from jax.sharding import PartitionSpec as P

QH = 32
KVH = 4
HD = 128
BLOCKS = 8
MESH = pl.DeviceIdType.MESH
F32 = jnp.float32
BF16 = jnp.bfloat16


def dot_nt(a, b):
    return lax.dot_general(a, b, (((1,), (1,)), ((), ())), preferred_element_type=F32)


def dot_nn(a, b):
    return lax.dot_general(a, b, (((1,), (0,)), ((), ())), preferred_element_type=F32)


def dot_tn(a, b):
    return lax.dot_general(a, b, (((0,), (0,)), ((), ())), preferred_element_type=F32)


def kernel(
    dp_n,
    seq_n,
    q_ref,
    k_ref,
    v_ref,
    len_ref,
    order_ref,
    g_ref,
    att_ref,
    gq_ref,
    gk_ref,
    gv_ref,
    kv_all,
    rows_in,
    stage,
    slots,
    halo,
    own_terms,
    back_out,
    back_in,
    start_s,
    count_s,
    s1_send,
    s1_recv,
    s2_send,
    s2_recv,
    halo_send,
    halo_recv,
    back_send,
    back_recv,
):
    tokens = q_ref.shape[0]
    loader_rows = tokens * seq_n
    capacity = loader_rows // dp_n
    per = capacity // tokens
    n = dp_n * per
    reach = loader_rows // BLOCKS // tokens
    qw = QH * HD // n
    heads = qw // HD
    kv_blocks = 2 * KVH
    repeat = n // kv_blocks
    docs = len_ref.shape[1]
    scale = HD ** (-0.5)
    d0 = lax.axis_index("dp")
    i0 = lax.axis_index("seq")
    source = i0 // per
    f_me = d0 * per + lax.rem(i0, per)

    def greet(t, carry):
        dd, ii = t // seq_n, lax.rem(t, seq_n)

        @pl.when(jnp.logical_or(dd != d0, ii != i0))
        def _():
            pl.semaphore_signal(
                pltpu.get_barrier_semaphore(), 1, device_id={"dp": dd, "seq": ii}, device_id_type=MESH
            )

        return carry

    lax.fori_loop(0, dp_n * seq_n, greet, 0)
    kv_all[:, : KVH * HD] = k_ref[...]
    kv_all[:, KVH * HD :] = v_ref[...]
    pl.semaphore_wait(pltpu.get_barrier_semaphore(), dp_n * seq_n - 1)

    def remote(src, dst, send, recv, dd, ii):
        return pltpu.make_async_remote_copy(
            src_ref=src,
            dst_ref=dst,
            send_sem=send,
            recv_sem=recv,
            device_id={"dp": dd, "seq": ii},
            device_id_type=MESH,
        )

    def start_copy(src, dst, send, recv, dd, ii):
        here = jnp.logical_and(dd == d0, ii == i0)

        @pl.when(here)
        def _():
            pltpu.make_async_copy(src, dst, recv).start()

        @pl.when(jnp.logical_not(here))
        def _():
            remote(src, dst, send, recv, dd, ii).start()

    def wait_sent(src, dst, send, recv, dd, ii):
        @pl.when(jnp.logical_or(dd != d0, ii != i0))
        def _():
            remote(src, dst, send, recv, dd, ii).wait_send()

    def wait_here(dst, recv):
        pltpu.make_async_copy(dst, dst, recv).wait()

    first = []
    my_rows = pl.ds(pl.multiple_of(i0 * tokens, tokens), tokens)
    for t in range(n):
        f = lax.rem(i0 + t, n)
        dd, ii = f // per, d0 * per + lax.rem(f, per)
        src_kv = kv_all.at[:, pl.ds(pl.multiple_of((f // repeat) * HD, HD), HD)]
        src_q = q_ref.at[:, pl.ds(pl.multiple_of(f * qw, HD), qw)]
        dst_kv = rows_in.at[my_rows, pl.ds(qw, HD)]
        dst_q = rows_in.at[my_rows, pl.ds(0, qw)]
        first.append((src_kv, dst_kv, s1_send.at[1, t], s1_recv.at[1, i0], dd, ii))
        first.append((src_q, dst_q, s1_send.at[0, t], s1_recv.at[0, i0], dd, ii))
        start_copy(*first[-2])
        start_copy(*first[-1])

    filled = []
    for b in range(dp_n):
        total = len_ref[b, 0]
        for d in range(1, docs):
            total = total + len_ref[b, d]
        filled.append(total)
    counts = [jnp.clip(x - source * capacity, 0, capacity) for x in filled]
    order = [order_ref[source, k] for k in range(dp_n)]
    place = []
    for b in range(dp_n):
        at = jnp.int32(0)
        for k in range(dp_n):
            at = at + jnp.where(order[k] == b, k, 0)
        place.append(at)
    for b in range(dp_n):
        at = jnp.int32(0)
        for c in range(dp_n):
            at = at + jnp.where(place[c] < place[b], counts[c], 0)
        start_s[b] = at
        count_s[b] = counts[b]

    row = lax.broadcasted_iota(jnp.int32, (tokens, 1), 0) + i0 * tokens
    low = jnp.zeros((tokens, 1), jnp.int32)
    end = jnp.int32(0)
    for d in range(docs):
        end = end + len_ref[d0, d]
        low = jnp.where(row >= end, end, low)
    is_filled = row < end
    low = jnp.where(is_filled, low, row)
    window = (reach + 1) * tokens
    col = lax.broadcasted_iota(jnp.int32, (tokens, window), 1) + (i0 - reach) * tokens
    allowed = jnp.logical_and(col >= low, col <= row)
    bias = jnp.where(allowed, 0.0, -jnp.inf).astype(F32)

    for d in range(1, reach + 1):

        @pl.when(i0 < d)
        def _():
            halo[d - 1] = jnp.zeros(halo.shape[1:], BF16)

    for j in range(seq_n):
        there = pl.ds(j * tokens, tokens)
        wait_here(rows_in.at[there, pl.ds(qw, HD)], s1_recv.at[1, j])
        wait_here(rows_in.at[there, pl.ds(0, qw)], s1_recv.at[0, j])

    second = []
    u = lax.broadcasted_iota(jnp.int32, (tokens, loader_rows), 0)
    r = lax.broadcasted_iota(jnp.int32, (tokens, loader_rows), 1)
    diff = r - u
    u_col = lax.broadcasted_iota(jnp.int32, (tokens, 1), 0)
    for t in range(n):
        f = lax.rem(f_me + t + 1, n)
        dd, h = f // per, lax.rem(f, per)
        ii = source * per + h
        offset = h * tokens
        target = jnp.where(u_col + offset < count_s[dd], start_s[dd] + offset, -2 * loader_rows)
        pick = jnp.where(diff == target, 1.0, 0.0).astype(BF16)
        stage[t] = dot_nn(pick, rows_in[...]).astype(BF16)
        item = (stage.at[t], slots.at[f_me], s2_send.at[t], s2_recv.at[f_me], dd, ii)
        second.append((item, None))
        start_copy(*item)
        for d in range(1, reach + 1):
            item = (
                stage.at[t, :, pl.ds(qw, HD)],
                halo.at[d - 1, f_me],
                halo_send.at[d - 1, t],
                halo_recv.at[d - 1, f_me],
                dd,
                ii + d,
            )
            second.append((item, ii + d < seq_n))

            @pl.when(ii + d < seq_n)
            def _():
                start_copy(*item)

    for f in range(n):
        wait_here(slots.at[f], s2_recv.at[f])
        for d in range(1, reach + 1):

            @pl.when(i0 >= d)
            def _():
                wait_here(halo.at[d - 1, f], halo_recv.at[d - 1, f])

    bias_all = jnp.concatenate([bias] * heads, axis=0) if heads > 1 else bias

    def stacked(x):
        return jnp.concatenate([x[:, a * HD : (a + 1) * HD] for a in range(heads)], axis=0) if heads > 1 else x

    def window_of(block):
        at = block * repeat
        parts = [halo[d - 1, at] for d in range(reach, 0, -1)]
        return jnp.concatenate(parts + [slots[at][:, qw:]], axis=0)

    per_group = n // KVH
    third = []
    for g in range(KVH):
        keys = window_of(g)
        values = window_of(KVH + g)
        k_terms = None
        for f in range(g * per_group, (g + 1) * per_group):
            query = stacked(slots[f][:, :qw])
            cot = stacked(jnp.where(is_filled, g_ref[:, f * qw : (f + 1) * qw], jnp.zeros((), BF16)))
            scores = dot_nt(query, keys) * scale + bias_all
            peak = jnp.max(scores, axis=-1, keepdims=True)
            e = jnp.exp(scores - peak)
            probs = e * (1.0 / jnp.sum(e, axis=-1, keepdims=True))
            half = probs.astype(BF16)
            att = dot_nn(half, values)
            gp = dot_nt(cot, values)
            row_dot = jnp.sum(cot.astype(F32) * att, axis=-1, keepdims=True)
            gs = (probs * (gp - row_dot)).astype(BF16)
            gq = dot_nn(gs, keys) * scale
            for a in range(heads):
                cols = slice(f * qw + a * HD, f * qw + (a + 1) * HD)
                att_ref[:, cols] = att[a * tokens : (a + 1) * tokens].astype(BF16)
                gq_ref[:, cols] = gq[a * tokens : (a + 1) * tokens].astype(BF16)
            kt, vt = dot_tn(gs, query), dot_tn(half, cot)
            k_terms, v_terms = (kt, vt) if k_terms is None else (k_terms + kt, v_terms + vt)
        terms = jnp.concatenate([k_terms * scale, v_terms], axis=1)
        own_terms[g] = terms[reach * tokens :]
        for d in range(1, reach + 1):
            back_out[d - 1, g] = terms[(reach - d) * tokens : (reach - d + 1) * tokens]
            item = (
                back_out.at[d - 1, g],
                back_in.at[d - 1, g],
                back_send.at[d - 1, g],
                back_recv.at[d - 1, g],
                d0,
                i0 - d,
            )
            third.append((item, d))

            @pl.when(i0 >= d)
            def _():
                remote(*item).start()

    for g in range(KVH):
        for d in range(1, reach + 1):

            @pl.when(i0 + d < seq_n)
            def _():
                wait_here(back_in.at[d - 1, g], back_recv.at[d - 1, g])
                own_terms[g] = own_terms[g] + back_in[d - 1, g]

        both = own_terms[g].astype(BF16)
        gk_ref[:, g * HD : (g + 1) * HD] = both[:, :HD]
        gv_ref[:, g * HD : (g + 1) * HD] = both[:, HD:]

    for item in first:
        wait_sent(*item)
    for item, ok in second:
        if ok is None:
            wait_sent(*item)
        else:

            @pl.when(ok)
            def _():
                wait_sent(*item)

    for item, d in third:

        @pl.when(i0 >= d)
        def _():
            remote(*item).wait_send()


def local(queries, keys, values, doc_lengths, loader_order, grad_out):
    dp_n = lax.axis_size("dp")
    seq_n = lax.axis_size("seq")
    tokens = queries.shape[0]
    loader_rows = tokens * seq_n
    per = seq_n // dp_n
    n = dp_n * per
    reach = loader_rows // BLOCKS // tokens
    qw = QH * HD // n
    vmem = pl.BlockSpec(memory_space=pltpu.VMEM)
    smem = pl.BlockSpec(memory_space=pltpu.SMEM)
    dma = pltpu.SemaphoreType.DMA
    return pl.pallas_call(
        functools.partial(kernel, dp_n, seq_n),
        out_shape=(
            jax.ShapeDtypeStruct(queries.shape, BF16),
            jax.ShapeDtypeStruct(queries.shape, BF16),
            jax.ShapeDtypeStruct(keys.shape, BF16),
            jax.ShapeDtypeStruct(keys.shape, BF16),
        ),
        in_specs=[vmem, vmem, vmem, smem, smem, vmem],
        out_specs=(vmem, vmem, vmem, vmem),
        scratch_shapes=[
            pltpu.VMEM((tokens, 2 * KVH * HD), BF16),
            pltpu.VMEM((loader_rows, qw + HD), BF16),
            pltpu.VMEM((n, tokens, qw + HD), BF16),
            pltpu.VMEM((n, tokens, qw + HD), BF16),
            pltpu.VMEM((reach, n, tokens, HD), BF16),
            pltpu.VMEM((KVH, tokens, 2 * HD), F32),
            pltpu.VMEM((reach, KVH, tokens, 2 * HD), F32),
            pltpu.VMEM((reach, KVH, tokens, 2 * HD), F32),
            pltpu.SMEM((dp_n,), jnp.int32),
            pltpu.SMEM((dp_n,), jnp.int32),
            dma((2, n)),
            dma((2, seq_n)),
            dma((n,)),
            dma((n,)),
            dma((reach, n)),
            dma((reach, n)),
            dma((reach, KVH)),
            dma((reach, KVH)),
        ],
        compiler_params=pltpu.CompilerParams(
            collective_id=0, has_side_effects=True, vmem_limit_bytes=56 * 2**20
        ),
        name="packed_attention",
    )(queries, keys, values, doc_lengths, loader_order, grad_out)


def solution(mesh):
    rows = P(("dp", "seq"), None)
    return jax.shard_map(
        local,
        mesh=mesh,
        in_specs=(rows, rows, rows, P(), P(), rows),
        out_specs=(rows, rows, rows, rows),
        check_vma=False,
    )
```

```python
import functools

import jax
import jax.numpy as jnp
from jax import lax
from jax.experimental import pallas as pl
from jax.experimental.pallas import tpu as pltpu
from jax.sharding import PartitionSpec as P

QH = 32
KVH = 4
HD = 128
BLOCKS = 8
MESH = pl.DeviceIdType.MESH
F32 = jnp.float32
BF16 = jnp.bfloat16


def dot_nt(a, b):
    return lax.dot_general(a, b, (((1,), (1,)), ((), ())), preferred_element_type=F32)


def dot_nn(a, b):
    return lax.dot_general(a, b, (((1,), (0,)), ((), ())), preferred_element_type=F32)


def dot_tn(a, b):
    return lax.dot_general(a, b, (((0,), (0,)), ((), ())), preferred_element_type=F32)


def kernel(
    dp_n,
    seq_n,
    chunks,
    q_ref,
    k_ref,
    v_ref,
    len_ref,
    order_ref,
    g_ref,
    att_ref,
    gq_ref,
    gk_ref,
    gv_ref,
    parts,
    middle,
    rows_in,
    pick,
    stage,
    slots,
    halo,
    terms_sum,
    back_in,
    start_s,
    count_s,
    h1_send,
    h1_recv,
    h2_send,
    h2_recv,
    h3_send,
    h3_recv,
    halo_send,
    halo_recv,
    back_send,
    back_recv,
):
    tokens = q_ref.shape[0]
    loader_rows = tokens * seq_n
    capacity = loader_rows // dp_n
    per = capacity // tokens
    n = dp_n * per
    reach = loader_rows // BLOCKS // tokens
    qw = QH * HD // n
    heads = qw // HD
    repeat = n // (2 * KVH)
    docs = len_ref.shape[1]
    scale = HD ** (-0.5)
    d0 = lax.axis_index("dp")
    i0 = lax.axis_index("seq")
    source = i0 // per
    plane = source * per
    f_me = d0 * per + lax.rem(i0, per)

    def greet(t, carry):
        dd, ii = t // seq_n, lax.rem(t, seq_n)
        its_plane = ii // per * per
        sends = jnp.logical_and(its_plane <= i0, i0 < its_plane + per + reach)
        other = jnp.logical_or(dd != d0, ii != i0)

        @pl.when(jnp.logical_and(other, jnp.logical_or(dd == d0, sends)))
        def _():
            pl.semaphore_signal(
                pltpu.get_barrier_semaphore(), 1, device_id={"dp": dd, "seq": ii}, device_id_type=MESH
            )

        return carry

    lax.fori_loop(0, dp_n * seq_n, greet, 0)
    for f in range(n):
        c = f // repeat
        src = k_ref if c < KVH else v_ref
        c = c % KVH
        parts[f // per, f % per, 0] = src[:, c * HD : (c + 1) * HD]
        for a in range(heads):
            parts[f // per, f % per, 1 + a] = q_ref[:, f * qw + a * HD : f * qw + (a + 1) * HD]
    last = jnp.minimum(plane + per + reach, seq_n)
    pl.semaphore_wait(pltpu.get_barrier_semaphore(), seq_n - 1 + (dp_n - 1) * (last - plane))

    def remote(src, dst, send, recv, dd, ii):
        return pltpu.make_async_remote_copy(
            src_ref=src,
            dst_ref=dst,
            send_sem=send,
            recv_sem=recv,
            device_id={"dp": dd, "seq": ii},
            device_id_type=MESH,
        )

    def start_copy(src, dst, send, recv, dd, ii):
        here = jnp.logical_and(dd == d0, ii == i0)

        @pl.when(here)
        def _():
            pltpu.make_async_copy(src, dst, recv).start()

        @pl.when(jnp.logical_not(here))
        def _():
            remote(src, dst, send, recv, dd, ii).start()

    def wait_sent(src, dst, send, recv, dd, ii):
        @pl.when(jnp.logical_or(dd != d0, ii != i0))
        def _():
            remote(src, dst, send, recv, dd, ii).wait_send()

    def wait_here(dst, recv):
        pltpu.make_async_copy(dst, dst, recv).wait()

    sent = []

    def hop1(c):
        u0, m = chunks[c]
        for t in range(1, dp_n + 1):
            dd = lax.rem(d0 + t, dp_n)
            item = (
                parts.at[dd, :, pl.ds(u0, m)],
                middle.at[d0, :, pl.ds(u0, m)],
                h1_send.at[c, t - 1],
                h1_recv.at[c, d0],
                dd,
                i0,
            )
            sent.append(item)
            start_copy(*item)

    def hop2(c):
        u0, m = chunks[c]
        for d in range(dp_n):
            wait_here(middle.at[d, :, pl.ds(u0, m)], h1_recv.at[c, d])
        for t in range(1, seq_n + 1):
            ii = lax.rem(i0 + t, seq_n)
            item = (
                middle.at[ii // per, lax.rem(ii, per), pl.ds(u0, m)],
                rows_in.at[pl.ds(u0, m), i0],
                h2_send.at[c, t - 1],
                h2_recv.at[c, i0],
                d0,
                ii,
            )
            sent.append(item)
            start_copy(*item)

    def hop3(c):
        u0, m = chunks[c]
        for j in range(seq_n):
            wait_here(rows_in.at[pl.ds(u0, m), j], h2_recv.at[c, j])
        rows = [rows_in[u0 + a].reshape(loader_rows, HD) for a in range(m)]
        rows = jnp.concatenate(rows, axis=1) if m > 1 else rows[0]
        block = min(n, 8)
        for f in range(0, n, block):
            placed = dot_nn(pick[f * tokens : (f + block) * tokens], rows).astype(BF16)
            for a in range(m):
                stage[u0 + a, f : f + block] = placed[:, a * HD : (a + 1) * HD].reshape(block, tokens, HD)
        for t in range(1, n + 1):
            f = lax.rem(f_me + t, n)
            dd, ii = f // per, plane + lax.rem(f, per)
            item = (
                stage.at[pl.ds(u0, m), f],
                slots.at[pl.ds(u0, m), f_me],
                h3_send.at[c, t - 1],
                h3_recv.at[c, f_me],
                dd,
                ii,
            )
            sent.append(item)
            start_copy(*item)
        if u0 == 0:
            for item, ok in halo_items():

                @pl.when(ok)
                def _():
                    start_copy(*item)

    def halo_items():
        items = []
        for t in range(1, n + 1):
            f = lax.rem(f_me + t, n)
            dd, ii = f // per, plane + lax.rem(f, per)
            for d in range(1, reach + 1):
                item = (
                    stage.at[0, f],
                    halo.at[d - 1, f_me],
                    halo_send.at[d - 1, t - 1],
                    halo_recv.at[d - 1, f_me],
                    dd,
                    ii + d,
                )
                items.append((item, ii + d < seq_n))
        return items

    hop1(0)
    if len(chunks) > 1:
        hop1(1)

    filled = []
    for b in range(dp_n):
        total = len_ref[b, 0]
        for d in range(1, docs):
            total = total + len_ref[b, d]
        filled.append(total)
    counts = [jnp.clip(x - source * capacity, 0, capacity) for x in filled]
    order = [order_ref[source, k] for k in range(dp_n)]
    place = []
    for b in range(dp_n):
        at = jnp.int32(0)
        for k in range(dp_n):
            at = at + jnp.where(order[k] == b, k, 0)
        place.append(at)
    for b in range(dp_n):
        at = jnp.int32(0)
        for c in range(dp_n):
            at = at + jnp.where(place[c] < place[b], counts[c], 0)
        start_s[b] = at
        count_s[b] = counts[b]

    u = lax.broadcasted_iota(jnp.int32, (tokens, loader_rows), 0)
    diff = lax.broadcasted_iota(jnp.int32, (tokens, loader_rows), 1) - u
    u_col = lax.broadcasted_iota(jnp.int32, (tokens, 1), 0)
    for f in range(n):
        offset = f % per * tokens
        b = f // per
        target = jnp.where(u_col + offset < count_s[b], start_s[b] + offset, -2 * loader_rows)
        pick[f * tokens : (f + 1) * tokens] = jnp.where(diff == target, 1.0, 0.0).astype(BF16)

    row = lax.broadcasted_iota(jnp.int32, (tokens, 1), 0) + i0 * tokens
    low = jnp.zeros((tokens, 1), jnp.int32)
    end = jnp.int32(0)
    for d in range(docs):
        end = end + len_ref[d0, d]
        low = jnp.where(row >= end, end, low)
    is_filled = row < end
    low = jnp.where(is_filled, low, row)
    window = (reach + 1) * tokens
    col = lax.broadcasted_iota(jnp.int32, (tokens, window), 1) + (i0 - reach) * tokens
    allowed = jnp.logical_and(col >= low, col <= row)
    bias = jnp.where(allowed, 0.0, -jnp.inf).astype(F32)

    for d in range(1, reach + 1):

        @pl.when(i0 < d)
        def _():
            halo[d - 1] = jnp.zeros(halo.shape[1:], BF16)

    terms_sum[...] = jnp.zeros(terms_sum.shape, F32)
    per_group = n // KVH

    def window_of(block):
        at = block * repeat
        return jnp.concatenate([halo[d - 1, at] for d in range(reach, 0, -1)] + [slots[0, at]], axis=0)

    def attend(c):
        u0, m = chunks[c]
        for f in range(n):
            wait_here(slots.at[pl.ds(u0, m), f], h3_recv.at[c, f])
        if u0 == 0:
            for f in range(n):
                for d in range(1, reach + 1):

                    @pl.when(i0 >= d)
                    def _():
                        wait_here(halo.at[d - 1, f], halo_recv.at[d - 1, f])

        units = [a for a in range(u0, u0 + m) if a > 0]
        for g in range(KVH if units else 0):
            keys = window_of(g)
            values = window_of(KVH + g)
            pairs = [(f, a) for f in range(g * per_group, (g + 1) * per_group) for a in units]
            for at in range(0, len(pairs), 4):
                attend_heads(g, keys, values, pairs[at : at + 4])
            if u0 + m == heads + 1:
                send_back(g)

    def attend_heads(g, keys, values, pairs):
        h = len(pairs)
        cols = [slice(f * qw + (a - 1) * HD, f * qw + a * HD) for f, a in pairs]
        query = jnp.concatenate([slots[a, f] for f, a in pairs], axis=0)
        no = jnp.zeros((), BF16)
        cot = jnp.concatenate([jnp.where(is_filled, g_ref[:, x], no) for x in cols], axis=0)
        scores = dot_nt(query, keys) * scale + jnp.concatenate([bias] * h, axis=0)
        peak = jnp.max(scores, axis=-1, keepdims=True)
        e = jnp.exp(scores - peak)
        probs = e * (1.0 / jnp.sum(e, axis=-1, keepdims=True))
        half = probs.astype(BF16)
        att = dot_nn(half, values)
        gp = dot_nt(cot, values)
        row_dot = jnp.sum(cot.astype(F32) * att, axis=-1, keepdims=True)
        gs = (probs * (gp - row_dot)).astype(BF16)
        gq = dot_nn(gs, keys) * scale
        for at, x in enumerate(cols):
            att_ref[:, x] = att[at * tokens : (at + 1) * tokens].astype(BF16)
            gq_ref[:, x] = gq[at * tokens : (at + 1) * tokens].astype(BF16)
        terms_sum[g, :, :HD] += dot_tn(gs, query) * scale
        terms_sum[g, :, HD:] += dot_tn(half, cot)

    def back_item(d, g):
        return (
            terms_sum.at[g, pl.ds((reach - d) * tokens, tokens)],
            back_in.at[d - 1, g],
            back_send.at[d - 1, g],
            back_recv.at[d - 1, g],
            d0,
            i0 - d,
        )

    def send_back(g):
        for d in range(1, reach + 1):

            @pl.when(i0 >= d)
            def _():
                remote(*back_item(d, g)).start()

    steps = len(chunks)
    for step in range(steps + 2):
        if step < steps:
            hop2(step)
            if step + 2 < steps:
                hop1(step + 2)
        if 0 <= step - 1 < steps:
            hop3(step - 1)
        if 0 <= step - 2 < steps:
            attend(step - 2)

    for item in sent:
        wait_sent(*item)
    for item, ok in halo_items():

        @pl.when(ok)
        def _():
            wait_sent(*item)

    for g in range(KVH):
        for d in range(1, reach + 1):

            @pl.when(i0 + d < seq_n)
            def _():
                wait_here(back_in.at[d - 1, g], back_recv.at[d - 1, g])
                terms_sum[g, reach * tokens :] += back_in[d - 1, g]

        both = terms_sum[g, reach * tokens :].astype(BF16)
        gk_ref[:, g * HD : (g + 1) * HD] = both[:, :HD]
        gv_ref[:, g * HD : (g + 1) * HD] = both[:, HD:]

    for g in range(KVH):
        for d in range(1, reach + 1):

            @pl.when(i0 >= d)
            def _():
                remote(*back_item(d, g)).wait_send()


def local(queries, keys, values, doc_lengths, loader_order, grad_out):
    dp_n = lax.axis_size("dp")
    seq_n = lax.axis_size("seq")
    tokens = queries.shape[0]
    loader_rows = tokens * seq_n
    per = seq_n // dp_n
    n = dp_n * per
    reach = loader_rows // BLOCKS // tokens
    units = 1 + QH // n
    chunks = [(0, 1)] + [(u, min(2, units - u)) for u in range(1, units, 2)]
    steps = len(chunks)
    vmem = pl.BlockSpec(memory_space=pltpu.VMEM)
    smem = pl.BlockSpec(memory_space=pltpu.SMEM)
    dma = pltpu.SemaphoreType.DMA
    return pl.pallas_call(
        functools.partial(kernel, dp_n, seq_n, chunks),
        out_shape=(
            jax.ShapeDtypeStruct(queries.shape, BF16),
            jax.ShapeDtypeStruct(queries.shape, BF16),
            jax.ShapeDtypeStruct(keys.shape, BF16),
            jax.ShapeDtypeStruct(keys.shape, BF16),
        ),
        in_specs=[vmem, vmem, vmem, smem, smem, vmem],
        out_specs=(vmem, vmem, vmem, vmem),
        scratch_shapes=[
            pltpu.VMEM((dp_n, per, units, tokens, HD), BF16),
            pltpu.VMEM((dp_n, per, units, tokens, HD), BF16),
            pltpu.VMEM((units, seq_n, tokens, HD), BF16),
            pltpu.VMEM((n * tokens, loader_rows), BF16),
            pltpu.VMEM((units, n, tokens, HD), BF16),
            pltpu.VMEM((units, n, tokens, HD), BF16),
            pltpu.VMEM((reach, n, tokens, HD), BF16),
            pltpu.VMEM((KVH, (reach + 1) * tokens, 2 * HD), F32),
            pltpu.VMEM((reach, KVH, tokens, 2 * HD), F32),
            pltpu.SMEM((dp_n,), jnp.int32),
            pltpu.SMEM((dp_n,), jnp.int32),
            dma((steps, dp_n)),
            dma((steps, dp_n)),
            dma((steps, seq_n)),
            dma((steps, seq_n)),
            dma((steps, n)),
            dma((steps, n)),
            dma((reach, n)),
            dma((reach, n)),
            dma((reach, KVH)),
            dma((reach, KVH)),
        ],
        compiler_params=pltpu.CompilerParams(
            collective_id=0, has_side_effects=True, vmem_limit_bytes=60 * 2**20
        ),
        name="packed_attention",
    )(queries, keys, values, doc_lengths, loader_order, grad_out)


def solution(mesh):
    rows = P(("dp", "seq"), None)
    return jax.shard_map(
        local,
        mesh=mesh,
        in_specs=(rows, rows, rows, P(), P(), rows),
        out_specs=(rows, rows, rows, rows),
        check_vma=False,
    )
```

```python
import functools

import jax
import jax.numpy as jnp
from jax import lax
from jax.experimental import pallas as pl
from jax.experimental.pallas import tpu as pltpu
from jax.sharding import PartitionSpec as P

QH = 32
KVH = 4
HD = 128
BLOCKS = 8
MESH = pl.DeviceIdType.MESH
F32 = jnp.float32
BF16 = jnp.bfloat16


def dot_nt(a, b):
    return lax.dot_general(a, b, (((1,), (1,)), ((), ())), preferred_element_type=F32)


def dot_nn(a, b):
    return lax.dot_general(a, b, (((1,), (0,)), ((), ())), preferred_element_type=F32)


def dot_tn(a, b):
    return lax.dot_general(a, b, (((0,), (0,)), ((), ())), preferred_element_type=F32)


def kernel(
    dp_n,
    seq_n,
    chunks,
    q_ref,
    k_ref,
    v_ref,
    len_ref,
    order_ref,
    g_ref,
    att_ref,
    gq_ref,
    gk_ref,
    gv_ref,
    parts,
    middle,
    rows_in,
    pick,
    stage,
    slots,
    halo,
    terms_sum,
    back_out,
    back_in,
    start_s,
    count_s,
    h1_send,
    h1_recv,
    h2_send,
    h2_recv,
    h3_send,
    h3_recv,
    halo_send,
    halo_recv,
    back_send,
    back_recv,
):
    tokens = q_ref.shape[0]
    loader_rows = tokens * seq_n
    capacity = loader_rows // dp_n
    per = capacity // tokens
    n = dp_n * per
    reach = loader_rows // BLOCKS // tokens
    qw = QH * HD // n
    heads = qw // HD
    repeat = n // (2 * KVH)
    docs = len_ref.shape[1]
    scale = HD ** (-0.5)
    d0 = lax.axis_index("dp")
    i0 = lax.axis_index("seq")
    source = i0 // per
    plane = source * per
    f_me = d0 * per + lax.rem(i0, per)

    def greet(t, carry):
        dd, ii = t // seq_n, lax.rem(t, seq_n)
        its_plane = ii // per * per
        sends = jnp.logical_and(its_plane <= i0, i0 < its_plane + per + reach)
        other = jnp.logical_or(dd != d0, ii != i0)

        @pl.when(jnp.logical_and(other, jnp.logical_or(dd == d0, sends)))
        def _():
            pl.semaphore_signal(
                pltpu.get_barrier_semaphore(), 1, device_id={"dp": dd, "seq": ii}, device_id_type=MESH
            )

        return carry

    lax.fori_loop(0, dp_n * seq_n, greet, 0)
    for f in range(n):
        c = f // repeat
        src = k_ref if c < KVH else v_ref
        c = c % KVH
        parts[f // per, f % per, 0] = src[:, c * HD : (c + 1) * HD]
        for a in range(heads):
            parts[f // per, f % per, 1 + a] = q_ref[:, f * qw + a * HD : f * qw + (a + 1) * HD]
    last = jnp.minimum(plane + per + reach, seq_n)
    pl.semaphore_wait(pltpu.get_barrier_semaphore(), seq_n - 1 + (dp_n - 1) * (last - plane))

    def remote(src, dst, send, recv, dd, ii):
        return pltpu.make_async_remote_copy(
            src_ref=src,
            dst_ref=dst,
            send_sem=send,
            recv_sem=recv,
            device_id={"dp": dd, "seq": ii},
            device_id_type=MESH,
        )

    def start_copy(src, dst, send, recv, dd, ii):
        here = jnp.logical_and(dd == d0, ii == i0)

        @pl.when(here)
        def _():
            pltpu.make_async_copy(src, dst, recv).start()

        @pl.when(jnp.logical_not(here))
        def _():
            remote(src, dst, send, recv, dd, ii).start()

    def wait_sent(src, dst, send, recv, dd, ii):
        @pl.when(jnp.logical_or(dd != d0, ii != i0))
        def _():
            remote(src, dst, send, recv, dd, ii).wait_send()

    def wait_here(dst, recv):
        pltpu.make_async_copy(dst, dst, recv).wait()

    sent = []

    def hop1(c):
        u0, m = chunks[c]
        for t in range(1, dp_n + 1):
            dd = lax.rem(d0 + t, dp_n)
            item = (
                parts.at[dd, :, pl.ds(u0, m)],
                middle.at[d0, :, pl.ds(u0, m)],
                h1_send.at[c, t - 1],
                h1_recv.at[c, d0],
                dd,
                i0,
            )
            sent.append(item)
            start_copy(*item)

    def hop2(c):
        u0, m = chunks[c]
        for d in range(dp_n):
            wait_here(middle.at[d, :, pl.ds(u0, m)], h1_recv.at[c, d])
        for t in range(1, seq_n + 1):
            ii = lax.rem(i0 + seq_n // 2 + t, seq_n)
            item = (
                middle.at[ii // per, lax.rem(ii, per), pl.ds(u0, m)],
                rows_in.at[pl.ds(u0, m), i0],
                h2_send.at[c, t - 1],
                h2_recv.at[c, i0],
                d0,
                ii,
            )
            sent.append(item)
            start_copy(*item)

    def hop3(c):
        u0, m = chunks[c]
        for j in range(seq_n):
            wait_here(rows_in.at[pl.ds(u0, m), j], h2_recv.at[c, j])
        rows = [rows_in[u0 + a].reshape(loader_rows, HD) for a in range(m)]
        rows = jnp.concatenate(rows, axis=1) if m > 1 else rows[0]
        block = min(n, 8)
        for f in range(0, n, block):
            placed = dot_nn(pick[f * tokens : (f + block) * tokens], rows).astype(BF16)
            for a in range(m):
                stage[u0 + a, f : f + block] = placed[:, a * HD : (a + 1) * HD].reshape(block, tokens, HD)
        for t in range(1, n + 1):
            f = lax.rem(f_me + t, n)
            dd, ii = f // per, plane + lax.rem(f, per)
            item = (
                stage.at[pl.ds(u0, m), f],
                slots.at[pl.ds(u0, m), f_me],
                h3_send.at[c, t - 1],
                h3_recv.at[c, f_me],
                dd,
                ii,
            )
            sent.append(item)
            start_copy(*item)
        if u0 == 0:
            for item, ok in halo_items():

                @pl.when(ok)
                def _():
                    start_copy(*item)

    def halo_items():
        items = []
        for t in range(1, n + 1):
            f = lax.rem(f_me + t, n)
            dd, ii = f // per, plane + lax.rem(f, per)
            for d in range(1, reach + 1):
                item = (
                    stage.at[0, f],
                    halo.at[d - 1, f_me],
                    halo_send.at[d - 1, t - 1],
                    halo_recv.at[d - 1, f_me],
                    dd,
                    ii + d,
                )
                items.append((item, ii + d < seq_n))
        return items

    hop1(0)
    if len(chunks) > 1:
        hop1(1)

    filled = []
    for b in range(dp_n):
        total = len_ref[b, 0]
        for d in range(1, docs):
            total = total + len_ref[b, d]
        filled.append(total)
    counts = [jnp.clip(x - source * capacity, 0, capacity) for x in filled]
    order = [order_ref[source, k] for k in range(dp_n)]
    place = []
    for b in range(dp_n):
        at = jnp.int32(0)
        for k in range(dp_n):
            at = at + jnp.where(order[k] == b, k, 0)
        place.append(at)
    for b in range(dp_n):
        at = jnp.int32(0)
        for c in range(dp_n):
            at = at + jnp.where(place[c] < place[b], counts[c], 0)
        start_s[b] = at
        count_s[b] = counts[b]

    u = lax.broadcasted_iota(jnp.int32, (tokens, loader_rows), 0)
    diff = lax.broadcasted_iota(jnp.int32, (tokens, loader_rows), 1) - u
    u_col = lax.broadcasted_iota(jnp.int32, (tokens, 1), 0)
    for f in range(n):
        offset = f % per * tokens
        b = f // per
        target = jnp.where(u_col + offset < count_s[b], start_s[b] + offset, -2 * loader_rows)
        pick[f * tokens : (f + 1) * tokens] = jnp.where(diff == target, 1.0, 0.0).astype(BF16)

    row = lax.broadcasted_iota(jnp.int32, (tokens, 1), 0) + i0 * tokens
    low = jnp.zeros((tokens, 1), jnp.int32)
    end = jnp.int32(0)
    for d in range(docs):
        end = end + len_ref[d0, d]
        low = jnp.where(row >= end, end, low)
    is_filled = row < end
    low = jnp.where(is_filled, low, row)
    window = (reach + 1) * tokens
    col = lax.broadcasted_iota(jnp.int32, (tokens, window), 1) + (i0 - reach) * tokens
    allowed = jnp.logical_and(col >= low, col <= row)
    bias = jnp.where(allowed, 0.0, -jnp.inf).astype(F32)

    for d in range(1, reach + 1):

        @pl.when(i0 < d)
        def _():
            halo[d - 1] = jnp.zeros(halo.shape[1:], BF16)

    terms_sum[...] = jnp.zeros(terms_sum.shape, F32)
    per_group = n // KVH

    def window_of(block):
        at = block * repeat
        return jnp.concatenate([halo[d - 1, at] for d in range(reach, 0, -1)] + [slots[0, at]], axis=0)

    def attend(c):
        u0, m = chunks[c]
        for f in range(n):
            wait_here(slots.at[pl.ds(u0, m), f], h3_recv.at[c, f])
        if u0 == 0:
            for f in range(n):
                for d in range(1, reach + 1):

                    @pl.when(i0 >= d)
                    def _():
                        wait_here(halo.at[d - 1, f], halo_recv.at[d - 1, f])

        units = [a for a in range(u0, u0 + m) if a > 0]
        for g in range(KVH if units else 0):
            keys = window_of(g)
            values = window_of(KVH + g)
            pairs = [(f, a) for f in range(g * per_group, (g + 1) * per_group) for a in units]
            for at in range(0, len(pairs), 4):
                attend_heads(g, keys, values, pairs[at : at + 4])
            if u0 + m == heads + 1:
                send_back(g)

    def attend_heads(g, keys, values, pairs):
        h = len(pairs)
        cols = [slice(f * qw + (a - 1) * HD, f * qw + a * HD) for f, a in pairs]
        query = jnp.concatenate([slots[a, f] for f, a in pairs], axis=0)
        no = jnp.zeros((), BF16)
        cot = jnp.concatenate([jnp.where(is_filled, g_ref[:, x], no) for x in cols], axis=0)
        scores = dot_nt(query, keys) * scale + jnp.concatenate([bias] * h, axis=0)
        peak = jnp.max(scores, axis=-1, keepdims=True)
        e = jnp.exp(scores - peak)
        probs = e * (1.0 / jnp.sum(e, axis=-1, keepdims=True))
        half = probs.astype(BF16)
        att = dot_nn(half, values)
        gp = dot_nt(cot, values)
        row_dot = jnp.sum(cot.astype(F32) * att, axis=-1, keepdims=True)
        gs = (probs * (gp - row_dot)).astype(BF16)
        gq = dot_nn(gs, keys) * scale
        for at, x in enumerate(cols):
            att_ref[:, x] = att[at * tokens : (at + 1) * tokens].astype(BF16)
            gq_ref[:, x] = gq[at * tokens : (at + 1) * tokens].astype(BF16)
        terms_sum[g, :, :HD] += dot_tn(gs, query) * scale
        terms_sum[g, :, HD:] += dot_tn(half, cot)

    def back_item(d, g):
        return (
            back_out.at[d - 1, g],
            back_in.at[d - 1, g],
            back_send.at[d - 1, g],
            back_recv.at[d - 1, g],
            d0,
            i0 - d,
        )

    def send_back(g):
        for d in range(1, reach + 1):

            @pl.when(i0 >= d)
            def _():
                back_out[d - 1, g] = terms_sum[g, (reach - d) * tokens : (reach - d + 1) * tokens].astype(BF16)
                remote(*back_item(d, g)).start()

    steps = len(chunks)
    for step in range(steps + 2):
        if step < steps:
            hop2(step)
            if step + 2 < steps:
                hop1(step + 2)
        if 0 <= step - 1 < steps:
            hop3(step - 1)
        if 0 <= step - 2 < steps:
            attend(step - 2)

    for item in sent:
        wait_sent(*item)
    for item, ok in halo_items():

        @pl.when(ok)
        def _():
            wait_sent(*item)

    for g in range(KVH):
        for d in range(1, reach + 1):

            @pl.when(i0 + d < seq_n)
            def _():
                wait_here(back_in.at[d - 1, g], back_recv.at[d - 1, g])
                terms_sum[g, reach * tokens :] += back_in[d - 1, g].astype(F32)

        both = terms_sum[g, reach * tokens :].astype(BF16)
        gk_ref[:, g * HD : (g + 1) * HD] = both[:, :HD]
        gv_ref[:, g * HD : (g + 1) * HD] = both[:, HD:]

    for g in range(KVH):
        for d in range(1, reach + 1):

            @pl.when(i0 >= d)
            def _():
                remote(*back_item(d, g)).wait_send()


def local(queries, keys, values, doc_lengths, loader_order, grad_out):
    dp_n = lax.axis_size("dp")
    seq_n = lax.axis_size("seq")
    tokens = queries.shape[0]
    loader_rows = tokens * seq_n
    per = seq_n // dp_n
    n = dp_n * per
    reach = loader_rows // BLOCKS // tokens
    units = 1 + QH // n
    chunks = [(0, 1)] + [(u, min(2, units - u)) for u in range(1, units, 2)]
    steps = len(chunks)
    vmem = pl.BlockSpec(memory_space=pltpu.VMEM)
    smem = pl.BlockSpec(memory_space=pltpu.SMEM)
    dma = pltpu.SemaphoreType.DMA
    return pl.pallas_call(
        functools.partial(kernel, dp_n, seq_n, chunks),
        out_shape=(
            jax.ShapeDtypeStruct(queries.shape, BF16),
            jax.ShapeDtypeStruct(queries.shape, BF16),
            jax.ShapeDtypeStruct(keys.shape, BF16),
            jax.ShapeDtypeStruct(keys.shape, BF16),
        ),
        in_specs=[vmem, vmem, vmem, smem, smem, vmem],
        out_specs=(vmem, vmem, vmem, vmem),
        scratch_shapes=[
            pltpu.VMEM((dp_n, per, units, tokens, HD), BF16),
            pltpu.VMEM((dp_n, per, units, tokens, HD), BF16),
            pltpu.VMEM((units, seq_n, tokens, HD), BF16),
            pltpu.VMEM((n * tokens, loader_rows), BF16),
            pltpu.VMEM((units, n, tokens, HD), BF16),
            pltpu.VMEM((units, n, tokens, HD), BF16),
            pltpu.VMEM((reach, n, tokens, HD), BF16),
            pltpu.VMEM((KVH, (reach + 1) * tokens, 2 * HD), F32),
            pltpu.VMEM((reach, KVH, tokens, 2 * HD), BF16),
            pltpu.VMEM((reach, KVH, tokens, 2 * HD), BF16),
            pltpu.SMEM((dp_n,), jnp.int32),
            pltpu.SMEM((dp_n,), jnp.int32),
            dma((steps, dp_n)),
            dma((steps, dp_n)),
            dma((steps, seq_n)),
            dma((steps, seq_n)),
            dma((steps, n)),
            dma((steps, n)),
            dma((reach, n)),
            dma((reach, n)),
            dma((reach, KVH)),
            dma((reach, KVH)),
        ],
        compiler_params=pltpu.CompilerParams(
            collective_id=0, has_side_effects=True, vmem_limit_bytes=60 * 2**20
        ),
        name="packed_attention",
    )(queries, keys, values, doc_lengths, loader_order, grad_out)


def solution(mesh):
    rows = P(("dp", "seq"), None)
    return jax.shard_map(
        local,
        mesh=mesh,
        in_specs=(rows, rows, rows, P(), P(), rows),
        out_specs=(rows, rows, rows, rows),
        check_vma=False,
    )
```

```python
import functools

import jax
import jax.numpy as jnp
from jax import lax
from jax.experimental import pallas as pl
from jax.experimental.pallas import tpu as pltpu
from jax.sharding import PartitionSpec as P

QH = 32
KVH = 4
HD = 128
BLOCKS = 8
MESH = pl.DeviceIdType.MESH
F32 = jnp.float32
BF16 = jnp.bfloat16


def dot_nt(a, b):
    return lax.dot_general(a, b, (((1,), (1,)), ((), ())), preferred_element_type=F32)


def dot_nn(a, b):
    return lax.dot_general(a, b, (((1,), (0,)), ((), ())), preferred_element_type=F32)


def dot_tn(a, b):
    return lax.dot_general(a, b, (((0,), (0,)), ((), ())), preferred_element_type=F32)


def kernel(
    dp_n,
    seq_n,
    chunks,
    q_ref,
    k_ref,
    v_ref,
    len_ref,
    order_ref,
    g_ref,
    att_ref,
    gq_ref,
    gk_ref,
    gv_ref,
    parts,
    middle,
    rows_in,
    pick,
    stage,
    slots,
    halo,
    terms_sum,
    back_out,
    back_in,
    start_s,
    count_s,
    h1_send,
    h1_recv,
    h2_send,
    h2_recv,
    h3_send,
    h3_recv,
    halo_send,
    halo_recv,
    back_send,
    back_recv,
):
    tokens = q_ref.shape[0]
    loader_rows = tokens * seq_n
    capacity = loader_rows // dp_n
    per = capacity // tokens
    n = dp_n * per
    reach = loader_rows // BLOCKS // tokens
    qw = QH * HD // n
    heads = qw // HD
    repeat = n // (2 * KVH)
    docs = len_ref.shape[1]
    scale = HD ** (-0.5)
    d0 = lax.axis_index("dp")
    i0 = lax.axis_index("seq")
    source = i0 // per
    plane = source * per
    f_me = d0 * per + lax.rem(i0, per)

    def greet(t, carry):
        dd, ii = t // seq_n, lax.rem(t, seq_n)
        its_plane = ii // per * per
        sends = jnp.logical_and(its_plane <= i0, i0 < its_plane + per + reach)
        other = jnp.logical_or(dd != d0, ii != i0)

        @pl.when(jnp.logical_and(other, jnp.logical_or(dd == d0, sends)))
        def _():
            pl.semaphore_signal(
                pltpu.get_barrier_semaphore(), 1, device_id={"dp": dd, "seq": ii}, device_id_type=MESH
            )

        return carry

    lax.fori_loop(0, dp_n * seq_n, greet, 0)
    for f in range(n):
        c = f // repeat
        src = k_ref if c < KVH else v_ref
        c = c % KVH
        parts[f // per, f % per, 0] = src[:, c * HD : (c + 1) * HD]
        for a in range(heads):
            parts[f // per, f % per, 1 + a] = q_ref[:, f * qw + a * HD : f * qw + (a + 1) * HD]
    last = jnp.minimum(plane + per + reach, seq_n)
    pl.semaphore_wait(pltpu.get_barrier_semaphore(), seq_n - 1 + (dp_n - 1) * (last - plane))

    def remote(src, dst, send, recv, dd, ii):
        return pltpu.make_async_remote_copy(
            src_ref=src,
            dst_ref=dst,
            send_sem=send,
            recv_sem=recv,
            device_id={"dp": dd, "seq": ii},
            device_id_type=MESH,
        )

    def start_copy(src, dst, send, recv, dd, ii):
        here = jnp.logical_and(dd == d0, ii == i0)

        @pl.when(here)
        def _():
            pltpu.make_async_copy(src, dst, recv).start()

        @pl.when(jnp.logical_not(here))
        def _():
            remote(src, dst, send, recv, dd, ii).start()

    def wait_sent(src, dst, send, recv, dd, ii):
        @pl.when(jnp.logical_or(dd != d0, ii != i0))
        def _():
            remote(src, dst, send, recv, dd, ii).wait_send()

    def wait_here(dst, recv):
        pltpu.make_async_copy(dst, dst, recv).wait()

    sent = []

    def hop1(c):
        u0, m = chunks[c]
        for t in range(1, dp_n + 1):
            dd = lax.rem(d0 + t, dp_n)
            item = (
                parts.at[dd, :, pl.ds(u0, m)],
                middle.at[d0, :, pl.ds(u0, m)],
                h1_send.at[c, t - 1],
                h1_recv.at[c, d0],
                dd,
                i0,
            )
            sent.append(item)
            start_copy(*item)

    def hop2(c):
        u0, m = chunks[c]
        for t in range(1, seq_n + 1):
            d = lax.rem(d0 + dp_n - (t - 1) // per, dp_n)
            if (t - 1) % per == 0:
                wait_here(middle.at[d, :, pl.ds(u0, m)], h1_recv.at[c, d])
            ii = d * per + lax.rem(i0 + t, per)
            item = (
                middle.at[ii // per, lax.rem(ii, per), pl.ds(u0, m)],
                rows_in.at[pl.ds(u0, m), i0],
                h2_send.at[c, t - 1],
                h2_recv.at[c, i0],
                d0,
                ii,
            )
            sent.append(item)
            start_copy(*item)

    def hop3(c):
        u0, m = chunks[c]
        for j in range(seq_n):
            wait_here(rows_in.at[pl.ds(u0, m), j], h2_recv.at[c, j])
        rows = [rows_in[u0 + a].reshape(loader_rows, HD) for a in range(m)]
        rows = jnp.concatenate(rows, axis=1) if m > 1 else rows[0]
        block = min(n, 8)
        for f in range(0, n, block):
            placed = dot_nn(pick[f * tokens : (f + block) * tokens], rows).astype(BF16)
            for a in range(m):
                stage[u0 + a, f : f + block] = placed[:, a * HD : (a + 1) * HD].reshape(block, tokens, HD)
        for t in range(1, n + 1):
            f = lax.rem(f_me + t, n)
            dd, ii = f // per, plane + lax.rem(f, per)
            item = (
                stage.at[pl.ds(u0, m), f],
                slots.at[pl.ds(u0, m), f_me],
                h3_send.at[c, t - 1],
                h3_recv.at[c, f_me],
                dd,
                ii,
            )
            sent.append(item)
            start_copy(*item)
        if u0 == 0:
            for item, ok in halo_items():

                @pl.when(ok)
                def _():
                    start_copy(*item)

    def halo_items():
        items = []
        for t in range(1, n + 1):
            f = lax.rem(f_me + t, n)
            dd, ii = f // per, plane + lax.rem(f, per)
            for d in range(1, reach + 1):
                item = (
                    stage.at[0, f],
                    halo.at[d - 1, f_me],
                    halo_send.at[d - 1, t - 1],
                    halo_recv.at[d - 1, f_me],
                    dd,
                    ii + d,
                )
                items.append((item, ii + d < seq_n))
        return items

    hop1(0)
    if len(chunks) > 1:
        hop1(1)

    filled = []
    for b in range(dp_n):
        total = len_ref[b, 0]
        for d in range(1, docs):
            total = total + len_ref[b, d]
        filled.append(total)
    counts = [jnp.clip(x - source * capacity, 0, capacity) for x in filled]
    order = [order_ref[source, k] for k in range(dp_n)]
    place = []
    for b in range(dp_n):
        at = jnp.int32(0)
        for k in range(dp_n):
            at = at + jnp.where(order[k] == b, k, 0)
        place.append(at)
    for b in range(dp_n):
        at = jnp.int32(0)
        for c in range(dp_n):
            at = at + jnp.where(place[c] < place[b], counts[c], 0)
        start_s[b] = at
        count_s[b] = counts[b]

    u = lax.broadcasted_iota(jnp.int32, (tokens, loader_rows), 0)
    diff = lax.broadcasted_iota(jnp.int32, (tokens, loader_rows), 1) - u
    u_col = lax.broadcasted_iota(jnp.int32, (tokens, 1), 0)
    for f in range(n):
        offset = f % per * tokens
        b = f // per
        target = jnp.where(u_col + offset < count_s[b], start_s[b] + offset, -2 * loader_rows)
        pick[f * tokens : (f + 1) * tokens] = jnp.where(diff == target, 1.0, 0.0).astype(BF16)

    row = lax.broadcasted_iota(jnp.int32, (tokens, 1), 0) + i0 * tokens
    low = jnp.zeros((tokens, 1), jnp.int32)
    end = jnp.int32(0)
    for d in range(docs):
        end = end + len_ref[d0, d]
        low = jnp.where(row >= end, end, low)
    is_filled = row < end
    low = jnp.where(is_filled, low, row)
    window = (reach + 1) * tokens
    col = lax.broadcasted_iota(jnp.int32, (tokens, window), 1) + (i0 - reach) * tokens
    allowed = jnp.logical_and(col >= low, col <= row)
    bias = jnp.where(allowed, 0.0, -jnp.inf).astype(F32)

    for d in range(1, reach + 1):

        @pl.when(i0 < d)
        def _():
            halo[d - 1] = jnp.zeros(halo.shape[1:], BF16)

    terms_sum[...] = jnp.zeros(terms_sum.shape, F32)
    per_group = n // KVH

    def window_of(block):
        at = block * repeat
        return jnp.concatenate([halo[d - 1, at] for d in range(reach, 0, -1)] + [slots[0, at]], axis=0)

    def attend(c):
        u0, m = chunks[c]
        for f in range(n):
            wait_here(slots.at[pl.ds(u0, m), f], h3_recv.at[c, f])
        if u0 == 0:
            for f in range(n):
                for d in range(1, reach + 1):

                    @pl.when(i0 >= d)
                    def _():
                        wait_here(halo.at[d - 1, f], halo_recv.at[d - 1, f])

        units = [a for a in range(u0, u0 + m) if a > 0]
        for g in range(KVH if units else 0):
            keys = window_of(g)
            values = window_of(KVH + g)
            pairs = [(f, a) for f in range(g * per_group, (g + 1) * per_group) for a in units]
            for at in range(0, len(pairs), 4):
                attend_heads(g, keys, values, pairs[at : at + 4])
            if u0 + m == heads + 1:
                send_back(g)

    def attend_heads(g, keys, values, pairs):
        h = len(pairs)
        cols = [slice(f * qw + (a - 1) * HD, f * qw + a * HD) for f, a in pairs]
        query = jnp.concatenate([slots[a, f] for f, a in pairs], axis=0)
        no = jnp.zeros((), BF16)
        cot = jnp.concatenate([jnp.where(is_filled, g_ref[:, x], no) for x in cols], axis=0)
        scores = dot_nt(query, keys) * scale + jnp.concatenate([bias] * h, axis=0)
        peak = jnp.max(scores, axis=-1, keepdims=True)
        e = jnp.exp(scores - peak)
        probs = e * (1.0 / jnp.sum(e, axis=-1, keepdims=True))
        half = probs.astype(BF16)
        att = dot_nn(half, values)
        gp = dot_nt(cot, values)
        row_dot = jnp.sum(cot.astype(F32) * att, axis=-1, keepdims=True)
        gs = (probs * (gp - row_dot)).astype(BF16)
        gq = dot_nn(gs, keys) * scale
        for at, x in enumerate(cols):
            att_ref[:, x] = att[at * tokens : (at + 1) * tokens].astype(BF16)
            gq_ref[:, x] = gq[at * tokens : (at + 1) * tokens].astype(BF16)
        terms_sum[g, :, :HD] += dot_tn(gs, query) * scale
        terms_sum[g, :, HD:] += dot_tn(half, cot)

    def back_item(d, g):
        return (
            back_out.at[d - 1, g],
            back_in.at[d - 1, g],
            back_send.at[d - 1, g],
            back_recv.at[d - 1, g],
            d0,
            i0 - d,
        )

    def send_back(g):
        for d in range(1, reach + 1):

            @pl.when(i0 >= d)
            def _():
                back_out[d - 1, g] = terms_sum[g, (reach - d) * tokens : (reach - d + 1) * tokens].astype(BF16)
                remote(*back_item(d, g)).start()

    steps = len(chunks)
    for step in range(steps + 2):
        if step < steps:
            hop2(step)
            if step + 2 < steps:
                hop1(step + 2)
        if 0 <= step - 1 < steps:
            hop3(step - 1)
        if 0 <= step - 2 < steps:
            attend(step - 2)

    for item in sent:
        wait_sent(*item)
    for item, ok in halo_items():

        @pl.when(ok)
        def _():
            wait_sent(*item)

    for g in range(KVH):
        for d in range(1, reach + 1):

            @pl.when(i0 + d < seq_n)
            def _():
                wait_here(back_in.at[d - 1, g], back_recv.at[d - 1, g])
                terms_sum[g, reach * tokens :] += back_in[d - 1, g].astype(F32)

        both = terms_sum[g, reach * tokens :].astype(BF16)
        gk_ref[:, g * HD : (g + 1) * HD] = both[:, :HD]
        gv_ref[:, g * HD : (g + 1) * HD] = both[:, HD:]

    for g in range(KVH):
        for d in range(1, reach + 1):

            @pl.when(i0 >= d)
            def _():
                remote(*back_item(d, g)).wait_send()


def local(queries, keys, values, doc_lengths, loader_order, grad_out):
    dp_n = lax.axis_size("dp")
    seq_n = lax.axis_size("seq")
    tokens = queries.shape[0]
    loader_rows = tokens * seq_n
    per = seq_n // dp_n
    n = dp_n * per
    reach = loader_rows // BLOCKS // tokens
    units = 1 + QH // n
    chunks = [(0, 1)] + [(u, min(2, units - u)) for u in range(1, units, 2)]
    steps = len(chunks)
    vmem = pl.BlockSpec(memory_space=pltpu.VMEM)
    smem = pl.BlockSpec(memory_space=pltpu.SMEM)
    dma = pltpu.SemaphoreType.DMA
    return pl.pallas_call(
        functools.partial(kernel, dp_n, seq_n, chunks),
        out_shape=(
            jax.ShapeDtypeStruct(queries.shape, BF16),
            jax.ShapeDtypeStruct(queries.shape, BF16),
            jax.ShapeDtypeStruct(keys.shape, BF16),
            jax.ShapeDtypeStruct(keys.shape, BF16),
        ),
        in_specs=[vmem, vmem, vmem, smem, smem, vmem],
        out_specs=(vmem, vmem, vmem, vmem),
        scratch_shapes=[
            pltpu.VMEM((dp_n, per, units, tokens, HD), BF16),
            pltpu.VMEM((dp_n, per, units, tokens, HD), BF16),
            pltpu.VMEM((units, seq_n, tokens, HD), BF16),
            pltpu.VMEM((n * tokens, loader_rows), BF16),
            pltpu.VMEM((units, n, tokens, HD), BF16),
            pltpu.VMEM((units, n, tokens, HD), BF16),
            pltpu.VMEM((reach, n, tokens, HD), BF16),
            pltpu.VMEM((KVH, (reach + 1) * tokens, 2 * HD), F32),
            pltpu.VMEM((reach, KVH, tokens, 2 * HD), BF16),
            pltpu.VMEM((reach, KVH, tokens, 2 * HD), BF16),
            pltpu.SMEM((dp_n,), jnp.int32),
            pltpu.SMEM((dp_n,), jnp.int32),
            dma((steps, dp_n)),
            dma((steps, dp_n)),
            dma((steps, seq_n)),
            dma((steps, seq_n)),
            dma((steps, n)),
            dma((steps, n)),
            dma((reach, n)),
            dma((reach, n)),
            dma((reach, KVH)),
            dma((reach, KVH)),
        ],
        compiler_params=pltpu.CompilerParams(
            collective_id=0, has_side_effects=True, vmem_limit_bytes=60 * 2**20
        ),
        name="packed_attention",
    )(queries, keys, values, doc_lengths, loader_order, grad_out)


def solution(mesh):
    rows = P(("dp", "seq"), None)
    return jax.shard_map(
        local,
        mesh=mesh,
        in_specs=(rows, rows, rows, P(), P(), rows),
        out_specs=(rows, rows, rows, rows),
        check_vma=False,
    )
```
